256 devices in a mesh: row: 16 (over y_lo, z), col: 16 (over x, y_hi, core).
Axes of the slice: x: 4, y: 4 (y_hi: 2, y_lo: 2; y = y_hi * 2 + y_lo), z: 8, core: 2. Of those that a mesh axis runs over, the one named last changes fastest.
Arguments:
- features: bfloat16 [16, 16, 32, 1024], P('col', 'row'), may hold values from -6 to 6
- inv_scales: float32 [32], replicated, may hold values from 0.05 to 0.3
- inverse_tiles: bfloat16 [16, 16, 6, 1024, 1024], P('row', 'col'), may hold values from -6 to 6
- tile_list: int32 [16, 16, 6, 2], P('row', 'col'), may hold values from 0 to 255, as said below
- live_count: int32 [16, 16], P('row', 'col'), may hold values from 1 to 6
Outputs:
- feature_grad: float32 [16, 16, 32, 1024], P('col', 'row')
The draws below stay inside these ranges and needn't reach their ends.
Inputs may be any that keep to these rules, and one draw needn't show every extreme that they name: `tile_list`: the slot of grid position (r, c) holds a tile (I, J) with I mod 16 == r, J // 16 == c and J <= I; tiles may repeat.
All inputs are finite; a program needn't handle non-finite values.
Results may differ from the reference program's by a relative error of at most 0.0095.
Values may be sent and summed in bfloat16 or wider, within the bound.
No kernel may reach another device: no remote copies, remote signals or barrier semaphores. Data moves between devices by JAX's collectives and lax.ppermute only.
A program may use at most 128 MiB of HBM per device.

```python
import math
import jax
import jax.numpy as jnp
from jax import lax

F = 32
TB = 1024
TILE_DEV = 6
N_ROW = 16
N_COL = 16


def draw_tile_list(key, part):
    key = jax.random.fold_in(key, 11)
    first, second = jax.random.split(key)
    shape = (N_ROW, N_COL, TILE_DEV)
    rows = lax.broadcasted_iota(jnp.int32, shape, 0)
    cols = lax.broadcasted_iota(jnp.int32, shape, 1)
    upper = jnp.where(cols == N_COL - 1, rows + 1, N_ROW)
    offset = jax.random.randint(first, shape, 0, upper)
    column_block = cols * N_ROW + offset
    lowest = jnp.maximum((column_block - rows + N_ROW - 1) // N_ROW, 0)
    multiple = jax.random.randint(second, shape, lowest, N_COL)
    row_block = rows + N_ROW * multiple
    pairs = jnp.stack([row_block, column_block], axis=-1).astype(jnp.int32)
    pairs = pairs.at[0, 0, 0].set(jnp.zeros((2,), jnp.int32))
    last = N_ROW * N_COL - 1
    pairs = pairs.at[N_ROW - 1, N_COL - 1, 0].set(jnp.full((2,), last, jnp.int32))
    return pairs


def draw_live_count(key, part):
    key = jax.random.fold_in(key, 23)
    counts = jax.random.randint(key, (N_ROW, N_COL), 1, TILE_DEV + 1)
    counts = counts.at[0, 0].set(TILE_DEV)
    counts = counts.at[N_ROW - 1, N_COL - 1].set(1)
    return counts.astype(jnp.int32)


def steps_of(key, shape, cuts, low, top_value):
    gain, own = 1.0, jax.random.fold_in(key, 6)
    for position, blocks in cuts:
        steps = jnp.exp(jax.random.uniform(jax.random.fold_in(own, position), (blocks,), jnp.float32, low / len(cuts), top_value / len(cuts)))
        gain = gain * jnp.repeat(steps, shape[position] // blocks).reshape([-1 if axis == position else 1 for axis in range(len(shape))])
    return gain


def noise(own_key, dims, width, bound, pieces=(), held_as=jnp.bfloat16):
    result = jax.random.normal(own_key, dims, jnp.float32) * width
    if len(pieces) > 0:
        result = steps_of(own_key, dims, pieces, -0.22, 0.18) * result
    return jnp.clip(result, min=-bound, max=bound).astype(held_as)


def setup_inputs(seed: int = 0) -> dict:
    splits = jax.random.split(jax.random.key(seed), 6)
    return {
        "features": noise(splits[0], (N_COL, N_ROW, F, TB), 1.0, 6.0, ((0, 16), (1, 16))),
        "inv_scales": jnp.clip(jnp.exp(jax.random.uniform(splits[1], (F,), jnp.float32, math.log(0.05), math.log(0.3))), 0.05, 0.3),
        "inverse_tiles": noise(splits[2], (N_ROW, N_COL, TILE_DEV, TB, TB), 1.0, 6.0, ((0, 16), (1, 16))),
        "tile_list": draw_tile_list(jax.random.fold_in(splits[5], 71), 0),
        "live_count": draw_live_count(jax.random.fold_in(splits[5], 71), 0),
    }


def reference(features, inv_scales, inverse_tiles, tile_list, live_count):
    blocks = features.reshape(N_COL * N_ROW, F, TB)
    scaled = (inv_scales[None, :, None] * blocks.astype(jnp.float32)).astype(jnp.bfloat16)
    norms = lax.optimization_barrier(jnp.sum(jnp.square(scaled.astype(jnp.float32)), axis=1))
    total = N_ROW * N_COL * TILE_DEV
    flat_tiles = inverse_tiles.reshape(total, TB, TB)
    flat_list = tile_list.reshape(total, 2)
    slots = jnp.arange(total, dtype=jnp.int32) % TILE_DEV
    owners = jnp.arange(total, dtype=jnp.int32) // TILE_DEV
    lives = live_count.reshape(N_ROW * N_COL)

    def one_tile(accum, idx):

        def work(acc):
            ib = flat_list[idx, 0]
            jb = flat_list[idx, 1]
            ui = scaled[ib]
            uj = scaled[jb]
            cross = lax.dot_general(ui, uj, (((0,), (0,)), ((), ())), preferred_element_type=jnp.float32)
            dist = jnp.sqrt(jnp.maximum(norms[ib][:, None] + norms[jb][None, :] - 2.0 * cross, 0.0))
            mult = jnp.where(ib == jb, 1.0, 2.0).astype(jnp.float32)
            coeff = mult * flat_tiles[idx].astype(jnp.float32) * (-5.0 / 3.0) * (1.0 + jnp.sqrt(5.0) * dist) * jnp.exp(-jnp.sqrt(5.0) * dist)
            coeff_b = coeff.astype(jnp.bfloat16)
            zi = blocks[ib]
            zj = blocks[jb]
            row_term = zi.astype(jnp.float32) * lax.optimization_barrier(jnp.sum(coeff, axis=1))[None, :] - lax.dot_general(zj, coeff_b, (((1,), (1,)), ((), ())), preferred_element_type=jnp.float32)
            col_term = zj.astype(jnp.float32) * lax.optimization_barrier(jnp.sum(coeff, axis=0))[None, :] - jnp.dot(zi, coeff_b, preferred_element_type=jnp.float32)
            acc = acc.at[ib].add(row_term)
            acc = acc.at[jb].add(col_term)
            return acc
        accum = lax.cond(slots[idx] < lives[owners[idx]], work, lambda acc: acc, accum)
        return (accum, None)
    start = jnp.zeros((N_COL * N_ROW, F, TB), jnp.float32)
    accum, _ = lax.scan(one_tile, start, jnp.arange(total, dtype=jnp.int32))
    grad = jnp.square(inv_scales)[None, :, None] * accum
    return grad.reshape(N_COL, N_ROW, F, TB)
```

```python
import jax
import jax.numpy as jnp
from jax import lax
from jax.experimental import pallas as pl
from jax.experimental.pallas import tpu as pltpu
from jax.sharding import PartitionSpec as P

F, TB, S, N = 32, 1024, 6, 16
K = 48
CH = 256
ROOT5 = 5.0**0.5
LOG2E = 1.4426950408889634


def split3(q):
    a = q.astype(jnp.bfloat16)
    r = q - a.astype(jnp.float32)
    b = r.astype(jnp.bfloat16)
    c = (r - b.astype(jnp.float32)).astype(jnp.bfloat16)
    return jnp.concatenate([a, b, c], axis=0)


def tile_kernel(live_ref, list_ref, inv, rows, cols, tiles, rout, cout, w, sem, racc, cacc, lhs, rhs, zi1, zj1, cb):
    live = live_ref[0]

    def fetch(s):
        return pltpu.make_async_copy(tiles.at[s], w.at[s], sem.at[s])

    for s in range(S):

        @pl.when(s < live)
        def _():
            fetch(s).start()

    racc[...] = jnp.zeros(racc.shape, jnp.float32)
    cacc[...] = jnp.zeros(cacc.shape, jnp.float32)
    iv = inv[...]
    ones3 = jnp.ones((3, TB), jnp.bfloat16)
    zpad = jnp.zeros((K - F - 6, TB), jnp.bfloat16)
    onepad = (lax.broadcasted_iota(jnp.int32, (16, TB), 0) == 0).astype(jnp.bfloat16)

    @pl.loop(0, live)
    def _(s):
        big_i = list_ref[2 * s]
        big_j = list_ref[2 * s + 1]
        ib = lax.shift_right_logical(big_i, 4) & 15
        jb = big_j & 15
        scale = jnp.where(big_i == big_j, 1.0, 2.0) * (-5.0 / 3.0 * ROOT5)
        zi = rows[ib]
        zj = cols[jb]
        ui = (iv * zi.astype(jnp.float32)).astype(jnp.bfloat16)
        uj = (iv * zj.astype(jnp.float32)).astype(jnp.bfloat16)
        qi = jnp.sum(jnp.square(ui.astype(jnp.float32)), axis=0, keepdims=True)
        qj = jnp.sum(jnp.square(uj.astype(jnp.float32)), axis=0, keepdims=True)
        lhs[...] = jnp.concatenate([ui, split3(qi), ones3, zpad], axis=0).T
        rhs[...] = jnp.concatenate([uj * jnp.bfloat16(-2.0), ones3, split3(qj), zpad], axis=0)
        zi1[...] = jnp.concatenate([zi, onepad], axis=0)
        zj1[...] = jnp.concatenate([zj, onepad], axis=0)
        fetch(s).wait()
        for jc in range(TB // CH):
            js = pl.ds(jc * CH, CH)
            for ic in range(TB // CH):
                at = pl.ds(ic * CH, CH)
                sq = lax.dot_general(
                    lhs[at, :], rhs[:, js], (((1,), (0,)), ((), ())), preferred_element_type=jnp.float32
                )
                sq = jnp.maximum(sq, 1e-30)
                d = sq * lax.rsqrt(sq)
                e = jnp.exp2(d * (-ROOT5 * LOG2E))
                g = ((d + 1.0 / ROOT5) * e).astype(jnp.bfloat16)
                cb[at, js] = g * w[s, at, js]
        x = cb[...]
        rt = lax.dot_general(zj1[...], x, (((1,), (1,)), ((), ())), preferred_element_type=jnp.float32)
        ct = lax.dot_general(zi1[...], x, (((1,), (0,)), ((), ())), preferred_element_type=jnp.float32)
        racc[ib] += scale * (zi.astype(jnp.float32) * rt[F : F + 1] - rt[:F])
        cacc[jb] += scale * (zj.astype(jnp.float32) * ct[F : F + 1] - ct[:F])

    rout[...] = racc[...].astype(jnp.bfloat16)
    cout[...] = cacc[...].astype(jnp.bfloat16)


def tile_pass(live, tile_list, inv, rows, cols, tiles):
    smem = pl.BlockSpec(memory_space=pltpu.SMEM)
    vmem = pl.BlockSpec(memory_space=pltpu.VMEM)
    part = jax.ShapeDtypeStruct((N, F, TB), jnp.bfloat16)
    return pl.pallas_call(
        tile_kernel,
        out_shape=[part, part],
        in_specs=[smem, smem, vmem, vmem, vmem, pl.BlockSpec(memory_space=pl.ANY)],
        out_specs=[vmem, vmem],
        scratch_shapes=[
            pltpu.VMEM((S, TB, TB), jnp.bfloat16),
            pltpu.SemaphoreType.DMA((S,)),
            pltpu.VMEM((N, F, TB), jnp.float32),
            pltpu.VMEM((N, F, TB), jnp.float32),
            pltpu.VMEM((TB, K), jnp.bfloat16),
            pltpu.VMEM((K, TB), jnp.bfloat16),
            pltpu.VMEM((K, TB), jnp.bfloat16),
            pltpu.VMEM((K, TB), jnp.bfloat16),
            pltpu.VMEM((TB, TB), jnp.bfloat16),
        ],
        compiler_params=pltpu.CompilerParams(vmem_limit_bytes=48 * 1024 * 1024),
        name="tile_pass",
    )(live, tile_list, inv, rows, cols, tiles)


def gather(block, axis):
    copies = jnp.broadcast_to(block[None], (N, F, TB))
    return lax.all_to_all(copies, axis, 0, 0, tiled=True)


def scatter_sum(parts, axis):
    got = lax.all_to_all(parts, axis, 0, 0, tiled=True)
    return jnp.sum(got.astype(jnp.float32), axis=0)


def body(features, inv_scales, inverse_tiles, tile_list, live_count):
    mine = features[0, 0]
    rows = gather(mine, "col")
    cols = gather(mine, "row")
    rpart, cpart = tile_pass(
        live_count.reshape(1), tile_list.reshape(2 * S), inv_scales.reshape(F, 1), rows, cols, inverse_tiles[0, 0]
    )
    total = scatter_sum(rpart, "col") + scatter_sum(cpart, "row")
    return (jnp.square(inv_scales)[:, None] * total)[None, None]


def solution(mesh):
    return jax.shard_map(
        body,
        mesh=mesh,
        in_specs=(
            P("col", "row", None, None),
            P(),
            P("row", "col", None, None, None),
            P("row", "col", None, None),
            P("row", "col"),
        ),
        out_specs=P("col", "row", None, None),
        check_vma=False,
    )
```

```python
import jax
import jax.numpy as jnp
from jax import lax
from jax.experimental import pallas as pl
from jax.experimental.pallas import tpu as pltpu
from jax.sharding import PartitionSpec as P

F, TB, S, N = 32, 1024, 6, 16
HALF = N // 2
K = 48
CH = 256
ROOT5 = 5.0**0.5
LOG2E = 1.4426950408889634


def split3(q):
    a = q.astype(jnp.bfloat16)
    r = q - a.astype(jnp.float32)
    b = r.astype(jnp.bfloat16)
    c = (r - b.astype(jnp.float32)).astype(jnp.bfloat16)
    return jnp.concatenate([a, b, c], axis=0)


def tile_kernel(live_ref, list_ref, inv, rows, rows2, cols, tiles, rout, rout2, cout, w, sem, racc, cacc, lhs, rhs, zi1, zj1, cb):
    me = lax.axis_index("col")
    live = live_ref[0]

    def fetch(s):
        return pltpu.make_async_copy(tiles.at[s], w.at[s], sem.at[s])

    for s in range(S):

        @pl.when(s < live)
        def _():
            fetch(s).start()

    racc[...] = jnp.zeros(racc.shape, jnp.float32)
    cacc[...] = jnp.zeros(cacc.shape, jnp.float32)
    iv = inv[...]
    ones3 = jnp.ones((3, TB), jnp.bfloat16)
    zpad = jnp.zeros((K - F - 6, TB), jnp.bfloat16)
    onepad = (lax.broadcasted_iota(jnp.int32, (16, TB), 0) == 0).astype(jnp.bfloat16)

    zi1[F:] = onepad
    zj1[F:] = onepad

    @pl.loop(0, live)
    def _(s):
        big_i = list_ref[2 * s]
        big_j = list_ref[2 * s + 1]
        owner = lax.shift_right_logical(big_i, 4) & 15
        ib = col_slot(owner, me)
        jb = big_j & 15
        scale = jnp.where(big_i == big_j, 1.0, 2.0) * (-5.0 / 3.0 * ROOT5)
        mine = ib < HALF

        @pl.when(mine)
        def _():
            zi1[:F] = rows[ib & 7]

        @pl.when(jnp.logical_not(mine))
        def _():
            zi1[:F] = rows2[ib & 7]

        zi = zi1[:F]
        zj = cols[jb]
        ui = (iv * zi.astype(jnp.float32)).astype(jnp.bfloat16)
        uj = (iv * zj.astype(jnp.float32)).astype(jnp.bfloat16)
        qi = jnp.sum(jnp.square(ui.astype(jnp.float32)), axis=0, keepdims=True)
        qj = jnp.sum(jnp.square(uj.astype(jnp.float32)), axis=0, keepdims=True)
        lhs[...] = jnp.concatenate([ui, split3(qi), ones3, zpad], axis=0).T
        rhs[...] = jnp.concatenate([uj * jnp.bfloat16(-2.0), ones3, split3(qj), zpad], axis=0)
        zj1[:F] = zj
        fetch(s).wait()
        for jc in range(TB // CH):
            js = pl.ds(jc * CH, CH)
            for ic in range(TB // CH):
                at = pl.ds(ic * CH, CH)
                sq = lax.dot_general(
                    lhs[at, :], rhs[:, js], (((1,), (0,)), ((), ())), preferred_element_type=jnp.float32
                )
                sq = jnp.maximum(sq, 1e-30)
                d = sq * lax.rsqrt(sq)
                e = jnp.exp2(d * (-ROOT5 * LOG2E))
                g = ((d + 1.0 / ROOT5) * e).astype(jnp.bfloat16)
                cb[at, js] = g * w[s, at, js]
        x = cb[...]
        rt = lax.dot_general(zj1[...], x, (((1,), (1,)), ((), ())), preferred_element_type=jnp.float32)
        ct = lax.dot_general(zi1[...], x, (((1,), (0,)), ((), ())), preferred_element_type=jnp.float32)
        racc[ib] += scale * (zi.astype(jnp.float32) * rt[F : F + 1] - rt[:F])
        cacc[jb] += scale * (zj.astype(jnp.float32) * ct[F : F + 1] - ct[:F])

    rout[...] = racc[:HALF].astype(jnp.bfloat16)
    rout2[...] = racc[HALF:].astype(jnp.bfloat16)
    cout[...] = cacc[...].astype(jnp.bfloat16)


def tile_pass(live, tile_list, inv, rows, rows2, cols, tiles):
    smem = pl.BlockSpec(memory_space=pltpu.SMEM)
    vmem = pl.BlockSpec(memory_space=pltpu.VMEM)
    half = jax.ShapeDtypeStruct((HALF, F, TB), jnp.bfloat16)
    part = jax.ShapeDtypeStruct((N, F, TB), jnp.bfloat16)
    return pl.pallas_call(
        tile_kernel,
        out_shape=[half, half, part],
        in_specs=[smem, smem, vmem, vmem, vmem, vmem, pl.BlockSpec(memory_space=pl.ANY)],
        out_specs=[vmem, vmem, vmem],
        scratch_shapes=[
            pltpu.VMEM((S, TB, TB), jnp.bfloat16),
            pltpu.SemaphoreType.DMA((S,)),
            pltpu.VMEM((N, F, TB), jnp.float32),
            pltpu.VMEM((N, F, TB), jnp.float32),
            pltpu.VMEM((TB, K), jnp.bfloat16),
            pltpu.VMEM((K, TB), jnp.bfloat16),
            pltpu.VMEM((K, TB), jnp.bfloat16),
            pltpu.VMEM((K, TB), jnp.bfloat16),
            pltpu.VMEM((TB, TB), jnp.bfloat16),
        ],
        compiler_params=pltpu.CompilerParams(vmem_limit_bytes=48 * 1024 * 1024),
        name="tile_pass",
    )(live, tile_list, inv, rows, rows2, cols, tiles)


def move(x, to):
    return lax.ppermute(x, "col", [(i, to(i)) for i in range(N)])


def along(k):
    return lambda i: (i + 4 * k) % N


def col_slot(owner, me):
    return ((owner ^ me) & 1) * HALF + (((me - owner + (owner & 3) - (me & 3)) & 12) >> 1) + (((owner ^ me) >> 1) & 1)


def gather_col(block):
    pair = jnp.stack([block, move(block, lambda i: i ^ 2)])
    mine = jnp.concatenate([pair] + [move(pair, along(k)) for k in (1, 2, 3)])
    return mine, move(mine, lambda i: i ^ 1)


def scatter_col(mine, other):
    f32, bf16 = jnp.float32, jnp.bfloat16
    chip = (mine.astype(f32) + move(other, lambda i: i ^ 1).astype(f32)).astype(bf16)
    pair = chip[:2].astype(f32)
    for k in (1, 2, 3):
        pair += move(chip[2 * k : 2 * k + 2], along(-k)).astype(f32)
    return pair[0] + move(pair[1].astype(bf16), lambda i: i ^ 2).astype(f32)


def gather_row(block):
    copies = jnp.broadcast_to(block[None], (N, F, TB))
    return lax.all_to_all(copies, "row", 0, 0, tiled=True)


def scatter_row(parts):
    got = lax.all_to_all(parts, "row", 0, 0, tiled=True)
    return jnp.sum(got.astype(jnp.float32), axis=0)


def body(features, inv_scales, inverse_tiles, tile_list, live_count):
    block = features[0, 0]
    cols = gather_row(block)
    rows, rows2 = gather_col(block)
    rpart, rpart2, cpart = tile_pass(
        live_count.reshape(1), tile_list.reshape(2 * S), inv_scales.reshape(F, 1), rows, rows2, cols, inverse_tiles[0, 0]
    )
    total = scatter_row(cpart) + scatter_col(rpart, rpart2)
    return (jnp.square(inv_scales)[:, None] * total)[None, None]


def solution(mesh):
    return jax.shard_map(
        body,
        mesh=mesh,
        in_specs=(
            P("col", "row", None, None),
            P(),
            P("row", "col", None, None, None),
            P("row", "col", None, None),
            P("row", "col"),
        ),
        out_specs=P("col", "row", None, None),
        check_vma=False,
    )
```

```python
import jax
import jax.numpy as jnp
from jax import lax
from jax.experimental import pallas as pl
from jax.experimental.pallas import tpu as pltpu
from jax.sharding import PartitionSpec as P

F, TB, S, N = 32, 1024, 6, 16
HALF = N // 2
FH = F // 2
TJ = TB // 2
K = 48
SI, SUB, CJ = 512, 128, 256
NS = TB // SI
ROOT5 = 5.0**0.5
LOG2E = 1.4426950408889634
f32, bf16 = jnp.float32, jnp.bfloat16


def nn(a, b):
    return lax.dot_general(a, b, (((1,), (0,)), ((), ())), preferred_element_type=f32)


def nt(a, b):
    return lax.dot_general(a, b, (((1,), (1,)), ((), ())), preferred_element_type=f32)


def split3(q):
    a = q.astype(bf16)
    r = q - a.astype(f32)
    b = r.astype(bf16)
    c = (r - b.astype(f32)).astype(bf16)
    return jnp.concatenate([a, b, c], axis=0)


def scaled(iv, z):
    u = (iv * z.astype(f32)).astype(bf16)
    return u, split3(jnp.sum(jnp.square(u.astype(f32)), axis=0, keepdims=True))


def ones_row(width):
    return (lax.broadcasted_iota(jnp.int32, (K - F, width), 0) == 0).astype(bf16)


def row_place(list_ref, s):
    return col_slot(lax.shift_right_logical(list_ref[2 * s], 4) & 15, lax.axis_index("col"))


def prepare_rows(live_ref, list_ref, inv, near, far, lhs, zi1):
    iv = inv[...]

    @pl.loop(0, live_ref[0])
    def _(s):
        ib = row_place(list_ref, s)

        @pl.when(ib < HALF)
        def _():
            zi1[s, :F] = near[ib & 7]

        @pl.when(ib >= HALF)
        def _():
            zi1[s, :F] = far[ib & 7]

        zi1[s, F:] = ones_row(TB)
        u, q = scaled(iv, zi1[s, :F])
        pad = jnp.zeros((K - F - 6, TB), bf16)
        lhs[s] = jnp.concatenate([u, q, jnp.ones((3, TB), bf16), pad], axis=0).T


def tile_kernel(second, live_ref, list_ref, inv, lhs, zi1, cols, *refs):
    if second:
        swapped, carry, tiles, rout, rout2, cout, w, sem, cacc, rhs, zj1, cb, racc = refs
    else:
        tiles, racc, keep, send, w, sem, cacc, rhs, zj1, cb = refs
    y = lax.axis_index("row") >> 3
    mine, other = pl.multiple_of(y * FH, FH), pl.multiple_of((1 - y) * FH, FH)
    live = live_ref[0]

    def fetch(s):
        return pltpu.make_async_copy(tiles.at[s, :, pl.ds(TJ if second else 0, TJ)], w.at[s], sem.at[s])

    fetch(0).start()

    @pl.when(1 < live)
    def _():
        fetch(1).start()

    racc[...] = jnp.zeros(racc.shape, f32)
    cacc[...] = jnp.zeros(cacc.shape, f32)
    zj1[1] = jnp.zeros((K, TJ), bf16)
    cb[NS - 1] = jnp.zeros((SI, TJ), bf16)
    iv = inv[...]

    def slot(s):
        big_i, big_j = list_ref[2 * s], list_ref[2 * s + 1]
        scale = jnp.where(big_i == big_j, 1.0, 2.0) * (-5.0 / 3.0 * ROOT5)
        return row_place(list_ref, s), big_j & 15, scale

    def prepare(s, p):
        jb = list_ref[2 * s + 1] & 15
        if second:
            zj1[p, pl.ds(mine, FH)] = cols[jb, F:]
            zj1[p, pl.ds(other, FH)] = swapped[jb]
        else:
            zj1[p, :F] = cols[jb, :F]
        zj1[p, F:] = ones_row(TJ)
        u, q = scaled(iv, zj1[p, :F])
        pad = jnp.zeros((K - F - 6, TJ), bf16)
        rhs[p] = jnp.concatenate([u * bf16(-2.0), jnp.ones((3, TJ), bf16), q, pad], axis=0)

    def contract(n, jc, s, p, jb, scale):
        js = pl.ds(jc * CJ, CJ)
        x = cb[n, :, js]
        ct = nn(zi1[s, :, pl.ds(n * SI, SI)], x)
        cacc[jb, :, js] += scale * (zj1[p, :F, js].astype(f32) * ct[F : F + 1] - ct[:F])
        return nt(zj1[p, :, js], x)

    def finish(n, s, ib, scale, rt):
        at = pl.ds(n * SI, SI)
        racc[ib, :, at] += scale * (zi1[s, :F, at].astype(f32) * rt[F : F + 1] - rt[:F])

    prepare(0, 0)

    @pl.loop(0, live)
    def _(s):
        p = s & 1
        prev = jnp.maximum(s - 1, 0)
        now, old = slot(s), slot(prev)
        fetch(s).wait()

        @pl.when(s + 2 < live)
        def _():
            fetch(s + 2).start()

        for n in range(NS):
            m, t, q, (ib, jb, scale) = (n - 1, s, p, now) if n else (NS - 1, prev, 1 - p, old)
            rt = None
            for jc in range(TJ // CJ):
                part = contract(m, jc, t, q, jb, scale)
                rt = part if rt is None else rt + part
                js = pl.ds(jc * CJ, CJ)
                for h in range(SI // SUB):
                    at = pl.ds(n * SI + h * SUB, SUB)
                    sq = jnp.maximum(nn(lhs[s, at, :], rhs[p, :, js]), 1e-30)
                    d = sq * lax.rsqrt(sq)
                    e = jnp.exp2(d * (-ROOT5 * LOG2E))
                    g = ((d + 1.0 / ROOT5) * e).astype(bf16)
                    cb[n, h * SUB : (h + 1) * SUB, js] = g * w[s, at, js]
            finish(m, t, ib, scale, rt)
            if n == NS - 1:
                prepare(jnp.minimum(s + 1, live - 1), 1 - p)

    last = live - 1
    ib, jb, scale = slot(last)
    rt = None
    for jc in range(TJ // CJ):
        part = contract(NS - 1, jc, last, last & 1, jb, scale)
        rt = part if rt is None else rt + part
    finish(NS - 1, last, ib, scale, rt)
    if second:
        rout[...] = (racc[:HALF] + carry[:HALF]).astype(bf16)
        rout2[...] = (racc[HALF:] + carry[HALF:]).astype(bf16)
        cout[:, :F] = cacc[...].astype(bf16)
        cout[:, F:] = jnp.zeros((N, FH, TJ), bf16)
    else:
        keep[...] = cacc[:, pl.ds(mine, FH)]
        send[...] = cacc[:, pl.ds(other, FH)].astype(bf16)


SMEM = pl.BlockSpec(memory_space=pltpu.SMEM)
VMEM = pl.BlockSpec(memory_space=pltpu.VMEM)


def prepare_pass(live, tile_list, inv, near, far):
    return pl.pallas_call(
        prepare_rows,
        out_shape=[jax.ShapeDtypeStruct((S, TB, K), bf16), jax.ShapeDtypeStruct((S, K, TB), bf16)],
        in_specs=[SMEM, SMEM] + [VMEM] * 3,
        out_specs=[VMEM] * 2,
        compiler_params=pltpu.CompilerParams(vmem_limit_bytes=16 * 1024 * 1024),
        cost_estimate=pl.CostEstimate(flops=2 * 10**9, bytes_accessed=10**6, transcendentals=0),
        name="prepare_rows",
    )(live, tile_list, inv, near, far)


def tile_pass(second, tiles, *args):
    total = (N, F, TB)
    half = jax.ShapeDtypeStruct((HALF, F, TB), bf16)
    scratch = [
        pltpu.VMEM((S, TB, TJ), bf16),
        pltpu.SemaphoreType.DMA((S,)),
        pltpu.VMEM((N, F, TJ), f32),
        pltpu.VMEM((2, K, TJ), bf16),
        pltpu.VMEM((2, K, TJ), bf16),
        pltpu.VMEM((NS, SI, TJ), bf16),
    ]
    if second:
        outs = [half, half, jax.ShapeDtypeStruct((N, F + FH, TJ), bf16)]
        scratch.append(pltpu.VMEM(total, f32))
    else:
        outs = [jax.ShapeDtypeStruct(shape, t) for shape, t in ((total, f32), ((N, FH, TJ), f32), ((N, FH, TJ), bf16))]

    def run(*refs):
        tile_kernel(second, *refs)

    return pl.pallas_call(
        run,
        out_shape=outs,
        in_specs=[SMEM] * 2 + [VMEM] * (len(args) - 2) + [pl.BlockSpec(memory_space=pl.ANY)],
        out_specs=[VMEM] * len(outs),
        scratch_shapes=scratch,
        compiler_params=pltpu.CompilerParams(vmem_limit_bytes=44 * 1024 * 1024),
        cost_estimate=pl.CostEstimate(flops=10**10, bytes_accessed=10**7, transcendentals=0),
        name="second_half" if second else "first_half",
    )(*args, tiles)


def move(x, to):
    return lax.ppermute(x, "col", [(i, to(i)) for i in range(N)])


def along(k):
    return lambda i: (i + 4 * k) % N


def col_slot(owner, me):
    return ((owner ^ me) & 1) * HALF + (((me - owner + (owner & 3) - (me & 3)) & 12) >> 1) + (((owner ^ me) >> 1) & 1)


def gather_col(block):
    pair = jnp.stack([block, move(block, lambda i: i ^ 2)])
    mine = jnp.concatenate([pair] + [move(pair, along(k)) for k in (1, 2, 3)])
    return mine, move(mine, lambda i: i ^ 1)


def scatter_col(mine, other):
    chip = (mine.astype(f32) + move(other, lambda i: i ^ 1).astype(f32)).astype(bf16)
    pair = chip[:2].astype(f32)
    for k in (1, 2, 3):
        pair += move(chip[2 * k : 2 * k + 2], along(-k)).astype(f32)
    return pair[0] + move(pair[1].astype(bf16), lambda i: i ^ 2).astype(f32)


def swap_y(x):
    return lax.ppermute(x, "row", [(i, i ^ HALF) for i in range(N)])


def gather_row(block):
    whole = jnp.broadcast_to(block[None, :, :TJ], (2, F, TJ))
    part = block[:, TJ:].reshape(2, FH, TJ)
    copies = jnp.concatenate([whole, part], axis=1)
    copies = jnp.broadcast_to(copies[:, None], (2, HALF, F + FH, TJ)).reshape(N, F + FH, TJ)
    return lax.all_to_all(copies, "row", 0, 0, tiled=True)


def scatter_row(parts):
    got = lax.all_to_all(parts, "row", 0, 0, tiled=True).astype(f32)
    second = jnp.sum(got[:, :F], axis=0)
    first = jnp.sum(got[:, F:].reshape(2, HALF, FH, TJ), axis=1).reshape(F, TJ)
    return jnp.concatenate([first, second], axis=1)


def body(features, inv_scales, inverse_tiles, tile_list, live_count):
    block = features[0, 0]
    live, places, inv = live_count.reshape(1), tile_list.reshape(2 * S), inv_scales.reshape(F, 1)
    cols = gather_row(block)
    near, far = gather_col(block)
    lhs, zi1 = prepare_pass(live, places, inv, near, far)
    swapped = swap_y(cols[:, F:])
    tiles = inverse_tiles[0, 0]
    carry, keep, send = tile_pass(False, tiles, live, places, inv, lhs, zi1, cols)
    got = swap_y(send)
    rpart, rpart2, cpart = tile_pass(True, tiles, live, places, inv, lhs, zi1, cols, swapped, carry)
    pair = (keep + got.astype(f32)).astype(bf16)
    cpart = lax.dynamic_update_slice(cpart, pair, (0, F, 0))
    total = scatter_row(cpart) + scatter_col(rpart, rpart2)
    return (jnp.square(inv_scales)[:, None] * total)[None, None]


def solution(mesh):
    return jax.shard_map(
        body,
        mesh=mesh,
        in_specs=(
            P("col", "row", None, None),
            P(),
            P("row", "col", None, None, None),
            P("row", "col", None, None),
            P("row", "col"),
        ),
        out_specs=P("col", "row", None, None),
        check_vma=False,
    )
```

```python
import jax
import jax.numpy as jnp
from jax import lax
from jax.experimental import pallas as pl
from jax.experimental.pallas import tpu as pltpu
from jax.sharding import PartitionSpec as P

F, TB, S, N = 32, 1024, 6, 16
HALF = N // 2
FH = F // 2
TJ = TB // 2
K = 48
SI, SUB, CJ = 512, 128, 256
NS = TB // SI
ROOT5 = 5.0**0.5
LOG2E = 1.4426950408889634
f32, bf16 = jnp.float32, jnp.bfloat16


def nn(a, b):
    return lax.dot_general(a, b, (((1,), (0,)), ((), ())), preferred_element_type=f32)


def nt(a, b):
    return lax.dot_general(a, b, (((1,), (1,)), ((), ())), preferred_element_type=f32)


def split3(q):
    a = q.astype(bf16)
    r = q - a.astype(f32)
    b = r.astype(bf16)
    c = (r - b.astype(f32)).astype(bf16)
    return jnp.concatenate([a, b, c], axis=0)


def scaled(iv, z):
    u = (iv * z.astype(f32)).astype(bf16)
    return u, split3(jnp.sum(jnp.square(u.astype(f32)), axis=0, keepdims=True))


def ones_row(width):
    return (lax.broadcasted_iota(jnp.int32, (K - F, width), 0) == 0).astype(bf16)


def row_place(list_ref, s):
    return col_slot(lax.shift_right_logical(list_ref[2 * s], 4) & 15, lax.axis_index("col"))


def prepare_rows(live_ref, list_ref, inv, near, far, lhs, zi1):
    iv = inv[...]

    @pl.loop(0, live_ref[0])
    def _(s):
        ib = row_place(list_ref, s)

        @pl.when(ib < HALF)
        def _():
            zi1[s, :F] = near[ib & 7]

        @pl.when(ib >= HALF)
        def _():
            zi1[s, :F] = far[ib & 7]

        zi1[s, F:] = ones_row(TB)
        u, q = scaled(iv, zi1[s, :F])
        pad = jnp.zeros((K - F - 6, TB), bf16)
        lhs[s] = jnp.concatenate([u, q, jnp.ones((3, TB), bf16), pad], axis=0).T


def tile_kernel(second, live_ref, list_ref, inv, lhs, zi1, cols, *refs):
    if second:
        swapped, carry, tiles, rout, rout2, cout, w, sem, cacc, rhs, zj1, cb, racc = refs
    else:
        tiles, racc, keep, send, w, sem, cacc, rhs, zj1, cb = refs
    y = lax.axis_index("row") >> 3
    mine, other = pl.multiple_of(y * FH, FH), pl.multiple_of((1 - y) * FH, FH)
    live = live_ref[0]

    def fetch(s):
        return pltpu.make_async_copy(tiles.at[s, :, pl.ds(TJ if second else 0, TJ)], w.at[s], sem.at[s])

    fetch(0).start()

    @pl.when(1 < live)
    def _():
        fetch(1).start()

    racc[...] = carry[...] if second else jnp.zeros(racc.shape, f32)
    cacc[...] = jnp.zeros(cacc.shape, f32)
    zj1[1] = jnp.zeros((K, TJ), bf16)
    cb[NS - 1] = jnp.zeros((SI, TJ), bf16)
    iv = inv[...]

    def slot(s):
        big_i, big_j = list_ref[2 * s], list_ref[2 * s + 1]
        scale = jnp.where(big_i == big_j, 1.0, 2.0) * (-5.0 / 3.0 * ROOT5)
        return row_place(list_ref, s), big_j & 15, scale

    def prepare(s, p):
        jb = list_ref[2 * s + 1] & 15
        if second:
            zj1[p, pl.ds(mine, FH)] = cols[jb, F:]
            zj1[p, pl.ds(other, FH)] = swapped[jb]
        else:
            zj1[p, :F] = cols[jb, :F]
        zj1[p, F:] = ones_row(TJ)
        u, q = scaled(iv, zj1[p, :F])
        pad = jnp.zeros((K - F - 6, TJ), bf16)
        rhs[p] = jnp.concatenate([u * bf16(-2.0), jnp.ones((3, TJ), bf16), q, pad], axis=0)

    def contract(n, jc, s, p, jb, scale):
        js = pl.ds(jc * CJ, CJ)
        x = cb[n, :, js]
        ct = nn(zi1[s, :, pl.ds(n * SI, SI)], x)
        cacc[jb, :, js] += scale * (zj1[p, :F, js].astype(f32) * ct[F : F + 1] - ct[:F])
        return nt(zj1[p, :, js], x)

    def finish(n, s, ib, scale, rt):
        at = pl.ds(n * SI, SI)
        racc[ib, :, at] += scale * (zi1[s, :F, at].astype(f32) * rt[F : F + 1] - rt[:F])

    prepare(0, 0)

    @pl.loop(0, live)
    def _(s):
        p = s & 1
        prev = jnp.maximum(s - 1, 0)
        now, old = slot(s), slot(prev)
        fetch(s).wait()

        @pl.when(s + 2 < live)
        def _():
            fetch(s + 2).start()

        for n in range(NS):
            m, t, q, (ib, jb, scale) = (n - 1, s, p, now) if n else (NS - 1, prev, 1 - p, old)
            rt = None
            for jc in range(TJ // CJ):
                part = contract(m, jc, t, q, jb, scale)
                rt = part if rt is None else rt + part
                js = pl.ds(jc * CJ, CJ)
                for h in range(SI // SUB):
                    at = pl.ds(n * SI + h * SUB, SUB)
                    sq = jnp.maximum(nn(lhs[s, at, :], rhs[p, :, js]), 1e-30)
                    d = sq * lax.rsqrt(sq)
                    e = jnp.exp2(d * (-ROOT5 * LOG2E))
                    g = ((d + 1.0 / ROOT5) * e).astype(bf16)
                    cb[n, h * SUB : (h + 1) * SUB, js] = g * w[s, at, js]
            finish(m, t, ib, scale, rt)
            if n == NS - 1:
                prepare(jnp.minimum(s + 1, live - 1), 1 - p)

    last = live - 1
    ib, jb, scale = slot(last)
    rt = None
    for jc in range(TJ // CJ):
        part = contract(NS - 1, jc, last, last & 1, jb, scale)
        rt = part if rt is None else rt + part
    finish(NS - 1, last, ib, scale, rt)
    if second:
        rout[...] = racc[:HALF].astype(bf16)
        rout2[...] = racc[HALF:].astype(bf16)
        cout[:, :F] = cacc[...].astype(bf16)
    else:
        keep[...] = cacc[:, pl.ds(mine, FH)]
        send[...] = cacc[:, pl.ds(other, FH)].astype(bf16)


SMEM = pl.BlockSpec(memory_space=pltpu.SMEM)
VMEM = pl.BlockSpec(memory_space=pltpu.VMEM)


def prepare_pass(live, tile_list, inv, near, far):
    return pl.pallas_call(
        prepare_rows,
        out_shape=[jax.ShapeDtypeStruct((S, TB, K), bf16), jax.ShapeDtypeStruct((S, K, TB), bf16)],
        in_specs=[SMEM, SMEM] + [VMEM] * 3,
        out_specs=[VMEM] * 2,
        compiler_params=pltpu.CompilerParams(vmem_limit_bytes=16 * 1024 * 1024),
        cost_estimate=pl.CostEstimate(flops=2 * 10**9, bytes_accessed=10**6, transcendentals=0),
        name="prepare_rows",
    )(live, tile_list, inv, near, far)


def tile_pass(second, tiles, *args):
    total = (N, F, TB)
    half = jax.ShapeDtypeStruct((HALF, F, TB), bf16)
    scratch = [
        pltpu.VMEM((S, TB, TJ), bf16),
        pltpu.SemaphoreType.DMA((S,)),
        pltpu.VMEM((N, F, TJ), f32),
        pltpu.VMEM((2, K, TJ), bf16),
        pltpu.VMEM((2, K, TJ), bf16),
        pltpu.VMEM((NS, SI, TJ), bf16),
    ]
    if second:
        outs = [half, half, jax.ShapeDtypeStruct((N, F + FH, TJ), bf16)]
        scratch.append(pltpu.VMEM(total, f32))
    else:
        outs = [jax.ShapeDtypeStruct(shape, t) for shape, t in ((total, f32), ((N, FH, TJ), f32), ((N, FH, TJ), bf16))]

    def run(*refs):
        tile_kernel(second, *refs)

    return pl.pallas_call(
        run,
        out_shape=outs,
        in_specs=[SMEM] * 2 + [VMEM] * (len(args) - 2) + [pl.BlockSpec(memory_space=pl.ANY)],
        out_specs=[VMEM] * len(outs),
        scratch_shapes=scratch,
        compiler_params=pltpu.CompilerParams(vmem_limit_bytes=44 * 1024 * 1024),
        cost_estimate=pl.CostEstimate(flops=10**10, bytes_accessed=10**7, transcendentals=0),
        name="second_half" if second else "first_half",
    )(*args, tiles)


def move(x, to):
    return lax.ppermute(x, "col", [(i, to(i)) for i in range(N)])


def along(k):
    return lambda i: (i + 4 * k) % N


def col_slot(owner, me):
    return ((owner ^ me) & 1) * HALF + (((me - owner + (owner & 3) - (me & 3)) & 12) >> 1) + (((owner ^ me) >> 1) & 1)


def gather_col(block):
    pair = jnp.stack([block, move(block, lambda i: i ^ 2)])
    mine = jnp.concatenate([pair] + [move(pair, along(k)) for k in (1, 2, 3)])
    return mine, move(mine, lambda i: i ^ 1)


def scatter_col(mine, other):
    chip = (mine.astype(f32) + move(other, lambda i: i ^ 1).astype(f32)).astype(bf16)
    pair = chip[:2].astype(f32)
    for k in (1, 2, 3):
        pair += move(chip[2 * k : 2 * k + 2], along(-k)).astype(f32)
    return pair[0] + move(pair[1].astype(bf16), lambda i: i ^ 2).astype(f32)


def swap_y(x):
    return lax.ppermute(x, "row", [(i, i ^ HALF) for i in range(N)])


def spread(block, copies):
    for d in range(N):
        part = d // HALF * FH
        copies[d, :F] = block[:, :TJ]
        copies[d, F:] = block[part : part + FH, TJ:]


def echo(block, copies, same):
    same[...] = block[...]


def gather_row(block):
    copies = pl.pallas_call(
        spread,
        out_shape=jax.ShapeDtypeStruct((N, F + FH, TJ), bf16),
        in_specs=[VMEM],
        out_specs=VMEM,
        name="spread",
    )(block)
    same = pl.pallas_call(
        echo,
        out_shape=jax.ShapeDtypeStruct((F, TB), bf16),
        in_specs=[VMEM, pl.BlockSpec(memory_space=pl.ANY)],
        out_specs=VMEM,
        name="echo",
    )(block, copies)
    return lax.all_to_all(copies, "row", 0, 0, tiled=True), same


def scatter_row(parts):
    got = lax.all_to_all(parts, "row", 0, 0, tiled=True).astype(f32)
    second = jnp.sum(got[:, :F], axis=0)
    first = jnp.sum(got[:, F:].reshape(2, HALF, FH, TJ), axis=1).reshape(F, TJ)
    return jnp.concatenate([first, second], axis=1)


def body(features, inv_scales, inverse_tiles, tile_list, live_count):
    block = features[0, 0]
    live, places, inv = live_count.reshape(1), tile_list.reshape(2 * S), inv_scales.reshape(F, 1)
    cols, block = gather_row(block)
    near, far = gather_col(block)
    lhs, zi1 = prepare_pass(live, places, inv, near, far)
    swapped = swap_y(cols[:, F:])
    tiles = inverse_tiles[0, 0]
    carry, keep, send = tile_pass(False, tiles, live, places, inv, lhs, zi1, cols)
    got = swap_y(send)
    rpart, rpart2, cpart = tile_pass(True, tiles, live, places, inv, lhs, zi1, cols, swapped, carry)
    pair = (keep + got.astype(f32)).astype(bf16)
    cpart = lax.dynamic_update_slice(cpart, pair, (0, F, 0))
    total = scatter_row(cpart) + scatter_col(rpart, rpart2)
    return (jnp.square(inv_scales)[:, None] * total)[None, None]


def solution(mesh):
    return jax.shard_map(
        body,
        mesh=mesh,
        in_specs=(
            P("col", "row", None, None),
            P(),
            P("row", "col", None, None, None),
            P("row", "col", None, None),
            P("row", "col"),
        ),
        out_specs=P("col", "row", None, None),
        check_vma=False,
    )
```

```python
import jax
import jax.numpy as jnp
from jax import lax
from jax.experimental import pallas as pl
from jax.experimental.pallas import tpu as pltpu
from jax.sharding import PartitionSpec as P

F, TB, S, N = 32, 1024, 6, 16
HALF = N // 2
FH = F // 2
TJ = TB // 2
K = 48
SI, SUB, CJ = 512, 128, 256
NS = TB // SI
ROOT5 = 5.0**0.5
LOG2E = 1.4426950408889634
f32, bf16 = jnp.float32, jnp.bfloat16


def nn(a, b):
    return lax.dot_general(a, b, (((1,), (0,)), ((), ())), preferred_element_type=f32)


def nt(a, b):
    return lax.dot_general(a, b, (((1,), (1,)), ((), ())), preferred_element_type=f32)


def split3(q):
    a = q.astype(bf16)
    r = q - a.astype(f32)
    b = r.astype(bf16)
    c = (r - b.astype(f32)).astype(bf16)
    return jnp.concatenate([a, b, c], axis=0)


def scaled(iv, z):
    u = (iv * z.astype(f32)).astype(bf16)
    return u, split3(jnp.sum(jnp.square(u.astype(f32)), axis=0, keepdims=True))


def ones_row(width):
    return (lax.broadcasted_iota(jnp.int32, (K - F, width), 0) == 0).astype(bf16)


def row_place(list_ref, s):
    return col_slot(lax.shift_right_logical(list_ref[2 * s], 4) & 15, lax.axis_index("col"))


def prepare_rows(live_ref, list_ref, inv, near, far, lhs, zi1):
    iv = inv[...]

    @pl.loop(0, live_ref[0])
    def _(s):
        ib = row_place(list_ref, s)

        @pl.when(ib < HALF)
        def _():
            zi1[s, :F] = near[ib & 7]

        @pl.when(ib >= HALF)
        def _():
            zi1[s, :F] = far[ib & 7]

        zi1[s, F:] = ones_row(TB)
        u, q = scaled(iv, zi1[s, :F])
        pad = jnp.zeros((K - F - 6, TB), bf16)
        lhs[s] = jnp.concatenate([u, q, jnp.ones((3, TB), bf16), pad], axis=0).T


def tile_kernel(second, live_ref, list_ref, inv, lhs, cols, *refs):
    if second:
        zi1, swapped, carry, w, rout, rout2, cout, cacc, rhs, zj1, cb, racc = refs
    else:
        near, far, tiles, racc, keep, send, ahead, cacc, rhs, zj1, cb, w, sem, zi1 = refs
    y = lax.axis_index("row") >> 3
    mine, other = pl.multiple_of(y * FH, FH), pl.multiple_of((1 - y) * FH, FH)
    live = live_ref[0]

    def fetch(s):
        return pltpu.make_async_copy(tiles.at[s, :, pl.ds(0, TJ)], w.at[s], sem.at[s])

    def fetch_ahead(s):
        return pltpu.make_async_copy(tiles.at[s, :, pl.ds(TJ, TJ)], ahead.at[s], sem.at[S + s])

    if not second:
        fetch(0).start()

        @pl.when(1 < live)
        def _():
            fetch(1).start()


    racc[...] = carry[...] if second else jnp.zeros(racc.shape, f32)
    cacc[...] = jnp.zeros(cacc.shape, f32)
    zj1[1] = jnp.zeros((K, TJ), bf16)
    cb[NS - 1] = jnp.zeros((SI, TJ), bf16)
    iv = inv[...]

    def slot(s):
        big_i, big_j = list_ref[2 * s], list_ref[2 * s + 1]
        scale = jnp.where(big_i == big_j, 1.0, 2.0) * (-5.0 / 3.0 * ROOT5)
        return row_place(list_ref, s), big_j & 15, scale

    def prepare(s, p):
        if not second:
            place = row_place(list_ref, s)
            zi1[s, :F] = jnp.where(place < HALF, near[place & 7], far[place & 7])
            zi1[s, F:] = ones_row(TB)
        jb = list_ref[2 * s + 1] & 15
        if second:
            zj1[p, pl.ds(mine, FH)] = cols[jb, F:]
            zj1[p, pl.ds(other, FH)] = swapped[jb]
        else:
            zj1[p, :F] = cols[jb, :F]
        zj1[p, F:] = ones_row(TJ)
        u, q = scaled(iv, zj1[p, :F])
        pad = jnp.zeros((K - F - 6, TJ), bf16)
        rhs[p] = jnp.concatenate([u * bf16(-2.0), jnp.ones((3, TJ), bf16), q, pad], axis=0)

    def contract(n, jc, s, p, jb, scale):
        js = pl.ds(jc * CJ, CJ)
        x = cb[n, :, js]
        ct = nn(zi1[s, :, pl.ds(n * SI, SI)], x)
        cacc[jb, :, js] += scale * (zj1[p, :F, js].astype(f32) * ct[F : F + 1] - ct[:F])
        return nt(zj1[p, :, js], x)

    def finish(n, s, ib, scale, rt):
        at = pl.ds(n * SI, SI)
        racc[ib, :, at] += scale * (zi1[s, :F, at].astype(f32) * rt[F : F + 1] - rt[:F])

    prepare(0, 0)

    @pl.loop(0, live)
    def _(s):
        p = s & 1
        prev = jnp.maximum(s - 1, 0)
        now, old = slot(s), slot(prev)
        if not second:
            fetch(s).wait()

            @pl.when(s + 2 < live)
            def _():
                fetch(s + 2).start()

            fetch_ahead(s).start()

        for n in range(NS):
            m, t, q, (ib, jb, scale) = (n - 1, s, p, now) if n else (NS - 1, prev, 1 - p, old)
            rt = None
            for jc in range(TJ // CJ):
                part = contract(m, jc, t, q, jb, scale)
                rt = part if rt is None else rt + part
                js = pl.ds(jc * CJ, CJ)
                for h in range(SI // SUB):
                    at = pl.ds(n * SI + h * SUB, SUB)
                    sq = jnp.maximum(nn(lhs[s, at, :], rhs[p, :, js]), 1e-30)
                    d = sq * lax.rsqrt(sq)
                    e = jnp.exp2(d * (-ROOT5 * LOG2E))
                    g = ((d + 1.0 / ROOT5) * e).astype(bf16)
                    cb[n, h * SUB : (h + 1) * SUB, js] = g * w[s, at, js]
            finish(m, t, ib, scale, rt)
            if n == NS - 1:
                prepare(jnp.minimum(s + 1, live - 1), 1 - p)

    last = live - 1
    ib, jb, scale = slot(last)
    rt = None
    for jc in range(TJ // CJ):
        part = contract(NS - 1, jc, last, last & 1, jb, scale)
        rt = part if rt is None else rt + part
    finish(NS - 1, last, ib, scale, rt)
    if second:
        rout[...] = racc[:HALF].astype(bf16)
        rout2[...] = racc[HALF:].astype(bf16)
        cout[:, :F] = cacc[...].astype(bf16)
    else:
        keep[...] = cacc[:, pl.ds(mine, FH)]
        send[...] = cacc[:, pl.ds(other, FH)].astype(bf16)

        @pl.loop(0, live)
        def _(s):
            fetch_ahead(s).wait()


SMEM = pl.BlockSpec(memory_space=pltpu.SMEM)
VMEM = pl.BlockSpec(memory_space=pltpu.VMEM)


def prepare_pass(live, tile_list, inv, near, far):
    return pl.pallas_call(
        prepare_rows,
        out_shape=[jax.ShapeDtypeStruct((S, TB, K), bf16), jax.ShapeDtypeStruct((S, K, TB), bf16)],
        in_specs=[SMEM, SMEM] + [VMEM] * 3,
        out_specs=[VMEM] * 2,
        compiler_params=pltpu.CompilerParams(vmem_limit_bytes=16 * 1024 * 1024),
        cost_estimate=pl.CostEstimate(flops=2 * 10**9, bytes_accessed=10**6, transcendentals=0),
        name="prepare_rows",
    )(live, tile_list, inv, near, far)


def tile_pass(second, *args):
    total, tile = (N, F, TB), (S, TB, TJ)
    half = jax.ShapeDtypeStruct((HALF, F, TB), bf16)
    scratch = [
        pltpu.VMEM((N, F, TJ), f32),
        pltpu.VMEM((2, K, TJ), bf16),
        pltpu.VMEM((2, K, TJ), bf16),
        pltpu.VMEM((NS, SI, TJ), bf16),
    ]
    if second:
        outs = [half, half, jax.ShapeDtypeStruct((N, F + FH, TJ), bf16)]
        scratch.append(pltpu.VMEM(total, f32))
    else:
        scratch += [pltpu.VMEM(tile, bf16), pltpu.SemaphoreType.DMA((2 * S,)), pltpu.VMEM((S, K, TB), bf16)]
        outs = [(total, f32), ((N, FH, TJ), f32), ((N, FH, TJ), bf16), (tile, bf16)]
        outs = [jax.ShapeDtypeStruct(*out) for out in outs]

    def run(*refs):
        tile_kernel(second, *refs)

    return pl.pallas_call(
        run,
        out_shape=outs,
        in_specs=[SMEM] * 2 + [VMEM] * (len(args) - 3) + [VMEM if second else pl.BlockSpec(memory_space=pl.ANY)],
        out_specs=[VMEM] * len(outs),
        scratch_shapes=scratch,
        compiler_params=pltpu.CompilerParams(vmem_limit_bytes=40 * 1024 * 1024),
        cost_estimate=pl.CostEstimate(flops=10**10, bytes_accessed=10**7, transcendentals=0),
        name="second_half" if second else "first_half",
    )(*args)


def move(x, to):
    return lax.ppermute(x, "col", [(i, to(i)) for i in range(N)])


def along(k):
    return lambda i: (i + 4 * k) % N


def col_slot(owner, me):
    return ((owner ^ me) & 1) * HALF + (((me - owner + (owner & 3) - (me & 3)) & 12) >> 1) + (((owner ^ me) >> 1) & 1)


def gather_col(block):
    pair = jnp.stack([block, move(block, lambda i: i ^ 2)])
    mine = jnp.concatenate([pair] + [move(pair, along(k)) for k in (1, 2, 3)])
    return mine, move(mine, lambda i: i ^ 1)


def scatter_col(mine, other):
    chip = (mine.astype(f32) + move(other, lambda i: i ^ 1).astype(f32)).astype(bf16)
    pair = chip[:2].astype(f32)
    for k in (1, 2, 3):
        pair += move(chip[2 * k : 2 * k + 2], along(-k)).astype(f32)
    return pair[0] + move(pair[1].astype(bf16), lambda i: i ^ 2).astype(f32)


def swap_y(x):
    return lax.ppermute(x, "row", [(i, i ^ HALF) for i in range(N)])


def spread(block, copies):
    for d in range(N):
        part = d // HALF * FH
        copies[d, :F] = block[:, :TJ]
        copies[d, F:] = block[part : part + FH, TJ:]


def gather_row(block):
    copies = pl.pallas_call(
        spread,
        out_shape=jax.ShapeDtypeStruct((N, F + FH, TJ), bf16),
        in_specs=[VMEM],
        out_specs=VMEM,
        name="spread",
    )(block)
    return lax.all_to_all(copies, "row", 0, 0, tiled=True)


def scatter_row(parts):
    got = lax.all_to_all(parts, "row", 0, 0, tiled=True).astype(f32)
    second = jnp.sum(got[:, :F], axis=0)
    first = jnp.sum(got[:, F:].reshape(2, HALF, FH, TJ), axis=1).reshape(F, TJ)
    return jnp.concatenate([first, second], axis=1)


def body(features, inv_scales, inverse_tiles, tile_list, live_count):
    block = features[0, 0]
    live, places, inv = live_count.reshape(1), tile_list.reshape(2 * S), inv_scales.reshape(F, 1)
    cols = gather_row(block)
    near, far = gather_col(block)
    lhs, zi1 = prepare_pass(live, places, inv, near, far)
    swapped = swap_y(cols[:, F:])
    tiles = inverse_tiles[0, 0]
    carry, keep, send, ahead = tile_pass(False, live, places, inv, lhs, cols, near, far, tiles)
    got = swap_y(send)
    rpart, rpart2, cpart = tile_pass(True, live, places, inv, lhs, cols, zi1, swapped, carry, ahead)
    pair = (keep + got.astype(f32)).astype(bf16)
    cpart = lax.dynamic_update_slice(cpart, pair, (0, F, 0))
    total = scatter_row(cpart) + scatter_col(rpart, rpart2)
    return (jnp.square(inv_scales)[:, None] * total)[None, None]


def solution(mesh):
    return jax.shard_map(
        body,
        mesh=mesh,
        in_specs=(
            P("col", "row", None, None),
            P(),
            P("row", "col", None, None, None),
            P("row", "col", None, None),
            P("row", "col"),
        ),
        out_specs=P("col", "row", None, None),
        check_vma=False,
    )
```

```python
import jax
import jax.numpy as jnp
from jax import lax
from jax.experimental import pallas as pl
from jax.experimental.pallas import tpu as pltpu
from jax.sharding import PartitionSpec as P

F, TB, S, N = 32, 1024, 6, 16
HALF = N // 2
FH = F // 2
TJ = TB // 2
K = 48
SI, SUB, CJ = 512, 128, 256
NS = TB // SI
ROOT5 = 5.0**0.5
LOG2E = 1.4426950408889634
f32, bf16 = jnp.float32, jnp.bfloat16


def nn(a, b):
    return lax.dot_general(a, b, (((1,), (0,)), ((), ())), preferred_element_type=f32)


def nt(a, b):
    return lax.dot_general(a, b, (((1,), (1,)), ((), ())), preferred_element_type=f32)


def split3(q):
    a = q.astype(bf16)
    r = q - a.astype(f32)
    b = r.astype(bf16)
    c = (r - b.astype(f32)).astype(bf16)
    return jnp.concatenate([a, b, c], axis=0)


def scaled(iv, z):
    u = (iv * z.astype(f32)).astype(bf16)
    return u, split3(jnp.sum(jnp.square(u.astype(f32)), axis=0, keepdims=True))


def ones_row(width):
    return (lax.broadcasted_iota(jnp.int32, (K - F, width), 0) == 0).astype(bf16)


def row_place(list_ref, s):
    return col_slot(lax.shift_right_logical(list_ref[2 * s], 4) & 15, lax.axis_index("col"))


def prepare_rows(live_ref, list_ref, inv, near, far, lhs, zi1):
    iv = inv[...]

    @pl.loop(0, live_ref[0])
    def _(s):
        ib = row_place(list_ref, s)

        @pl.when(ib < HALF)
        def _():
            zi1[s, :F] = near[ib & 7]

        @pl.when(ib >= HALF)
        def _():
            zi1[s, :F] = far[ib & 7]

        zi1[s, F:] = ones_row(TB)
        u, q = scaled(iv, zi1[s, :F])
        pad = jnp.zeros((K - F - 6, TB), bf16)
        lhs[s] = jnp.concatenate([u, q, jnp.ones((3, TB), bf16), pad], axis=0).T


def tile_kernel(second, live_ref, list_ref, inv, lhs, cols, *refs):
    if second:
        zi1, swapped, carry, w, rout, rout2, cout, cacc, rhs, zj1, cb, racc = refs
    else:
        near, far, tiles, racc, keep, send, w, cacc, rhs, zj1, cb, sem, zi1 = refs
    y = lax.axis_index("row") >> 3
    mine, other = pl.multiple_of(y * FH, FH), pl.multiple_of((1 - y) * FH, FH)
    live = live_ref[0]
    start = TJ if second else 0

    def fetch(s):
        return pltpu.make_async_copy(tiles.at[s], w.at[s], sem.at[s])

    if not second:
        fetch(0).start()

    racc[...] = carry[...] if second else jnp.zeros(racc.shape, f32)
    cacc[...] = jnp.zeros(cacc.shape, f32)
    zj1[1] = jnp.zeros((K, TJ), bf16)
    cb[NS - 1] = jnp.zeros((SI, TJ), bf16)
    iv = inv[...]

    def slot(s):
        big_i, big_j = list_ref[2 * s], list_ref[2 * s + 1]
        scale = jnp.where(big_i == big_j, 1.0, 2.0) * (-5.0 / 3.0 * ROOT5)
        return row_place(list_ref, s), big_j & 15, scale

    def prepare(s, p):
        if not second:
            place = row_place(list_ref, s)
            zi1[s, :F] = jnp.where(place < HALF, near[place & 7], far[place & 7])
            zi1[s, F:] = ones_row(TB)
        jb = list_ref[2 * s + 1] & 15
        if second:
            zj1[p, pl.ds(mine, FH)] = cols[jb, F:]
            zj1[p, pl.ds(other, FH)] = swapped[jb]
        else:
            zj1[p, :F] = cols[jb, :F]
        zj1[p, F:] = ones_row(TJ)
        u, q = scaled(iv, zj1[p, :F])
        pad = jnp.zeros((K - F - 6, TJ), bf16)
        rhs[p] = jnp.concatenate([u * bf16(-2.0), jnp.ones((3, TJ), bf16), q, pad], axis=0)

    def contract(n, jc, s, p, jb, scale):
        js = pl.ds(jc * CJ, CJ)
        x = cb[n, :, js]
        ct = nn(zi1[s, :, pl.ds(n * SI, SI)], x)
        cacc[jb, :, js] += scale * (zj1[p, :F, js].astype(f32) * ct[F : F + 1] - ct[:F])
        return nt(zj1[p, :, js], x)

    def finish(n, s, ib, scale, rt):
        at = pl.ds(n * SI, SI)
        racc[ib, :, at] += scale * (zi1[s, :F, at].astype(f32) * rt[F : F + 1] - rt[:F])

    prepare(0, 0)

    if not second:

        @pl.when(1 < live)
        def _():
            fetch(1).start()

    @pl.loop(0, live)
    def _(s):
        p = s & 1
        prev = jnp.maximum(s - 1, 0)
        now, old = slot(s), slot(prev)
        if not second:
            fetch(s).wait()

            @pl.when(s + 2 < live)
            def _():
                fetch(s + 2).start()

        for n in range(NS):
            m, t, q, (ib, jb, scale) = (n - 1, s, p, now) if n else (NS - 1, prev, 1 - p, old)
            rt = None
            for jc in range(TJ // CJ):
                part = contract(m, jc, t, q, jb, scale)
                rt = part if rt is None else rt + part
                js = pl.ds(jc * CJ, CJ)
                for h in range(SI // SUB):
                    at = pl.ds(n * SI + h * SUB, SUB)
                    sq = jnp.maximum(nn(lhs[s, at, :], rhs[p, :, js]), 1e-30)
                    d = sq * lax.rsqrt(sq)
                    e = jnp.exp2(d * (-ROOT5 * LOG2E))
                    g = ((d + 1.0 / ROOT5) * e).astype(bf16)
                    cb[n, h * SUB : (h + 1) * SUB, js] = g * w[s, at, pl.ds(start + jc * CJ, CJ)]
            finish(m, t, ib, scale, rt)
            if n == NS - 1:
                prepare(jnp.minimum(s + 1, live - 1), 1 - p)

    last = live - 1
    ib, jb, scale = slot(last)
    rt = None
    for jc in range(TJ // CJ):
        part = contract(NS - 1, jc, last, last & 1, jb, scale)
        rt = part if rt is None else rt + part
    finish(NS - 1, last, ib, scale, rt)
    if second:
        rout[...] = racc[:HALF].astype(bf16)
        rout2[...] = racc[HALF:].astype(bf16)
        cout[:, :F] = cacc[...].astype(bf16)
    else:
        keep[...] = cacc[:, pl.ds(mine, FH)]
        send[...] = cacc[:, pl.ds(other, FH)].astype(bf16)


SMEM = pl.BlockSpec(memory_space=pltpu.SMEM)
VMEM = pl.BlockSpec(memory_space=pltpu.VMEM)


def prepare_pass(live, tile_list, inv, near, far):
    return pl.pallas_call(
        prepare_rows,
        out_shape=[jax.ShapeDtypeStruct((S, TB, K), bf16), jax.ShapeDtypeStruct((S, K, TB), bf16)],
        in_specs=[SMEM, SMEM] + [VMEM] * 3,
        out_specs=[VMEM] * 2,
        compiler_params=pltpu.CompilerParams(vmem_limit_bytes=16 * 1024 * 1024),
        cost_estimate=pl.CostEstimate(flops=2 * 10**9, bytes_accessed=10**6, transcendentals=0),
        name="prepare_rows",
    )(live, tile_list, inv, near, far)


def tile_pass(second, *args):
    total, tile = (N, F, TB), (S, TB, TB)
    half = jax.ShapeDtypeStruct((HALF, F, TB), bf16)
    scratch = [
        pltpu.VMEM((N, F, TJ), f32),
        pltpu.VMEM((2, K, TJ), bf16),
        pltpu.VMEM((2, K, TJ), bf16),
        pltpu.VMEM((NS, SI, TJ), bf16),
    ]
    if second:
        outs = [half, half, jax.ShapeDtypeStruct((N, F + FH, TJ), bf16)]
        scratch.append(pltpu.VMEM(total, f32))
    else:
        scratch += [pltpu.SemaphoreType.DMA((S,)), pltpu.VMEM((S, K, TB), bf16)]
        outs = [(total, f32), ((N, FH, TJ), f32), ((N, FH, TJ), bf16), (tile, bf16)]
        outs = [jax.ShapeDtypeStruct(*out) for out in outs]

    def run(*refs):
        tile_kernel(second, *refs)

    return pl.pallas_call(
        run,
        out_shape=outs,
        in_specs=[SMEM] * 2 + [VMEM] * (len(args) - 3) + [VMEM if second else pl.BlockSpec(memory_space=pl.ANY)],
        out_specs=[VMEM] * len(outs),
        scratch_shapes=scratch,
        compiler_params=pltpu.CompilerParams(vmem_limit_bytes=32 * 1024 * 1024),
        cost_estimate=pl.CostEstimate(flops=10**10, bytes_accessed=10**7, transcendentals=0),
        name="second_half" if second else "first_half",
    )(*args)


def move(x, to):
    return lax.ppermute(x, "col", [(i, to(i)) for i in range(N)])


def along(k):
    return lambda i: (i + 4 * k) % N


def col_slot(owner, me):
    return ((owner ^ me) & 1) * HALF + (((me - owner + (owner & 3) - (me & 3)) & 12) >> 1) + (((owner ^ me) >> 1) & 1)


def gather_col(block):
    pair = jnp.stack([block, move(block, lambda i: i ^ 2)])
    mine = jnp.concatenate([pair] + [move(pair, along(k)) for k in (1, 2, 3)])
    return mine, move(mine, lambda i: i ^ 1)


def scatter_col(mine, other):
    chip = (mine.astype(f32) + move(other, lambda i: i ^ 1).astype(f32)).astype(bf16)
    pair = chip[:2].astype(f32)
    for k in (1, 2, 3):
        pair += move(chip[2 * k : 2 * k + 2], along(-k)).astype(f32)
    return pair[0] + move(pair[1].astype(bf16), lambda i: i ^ 2).astype(f32)


def swap_y(x):
    return lax.ppermute(x, "row", [(i, i ^ HALF) for i in range(N)])


def gather_row(block):
    whole = jnp.broadcast_to(block[None, :, :TJ], (N, F, TJ))
    part = jnp.broadcast_to(block[:, TJ:].reshape(2, 1, FH, TJ), (2, HALF, FH, TJ)).reshape(N, FH, TJ)
    return lax.all_to_all(jnp.concatenate([whole, part], axis=1), "row", 0, 0, tiled=True)


def scatter_row(parts):
    got = lax.all_to_all(parts, "row", 0, 0, tiled=True).astype(f32)
    second = jnp.sum(got[:, :F], axis=0)
    first = jnp.sum(got[:, F:].reshape(2, HALF, FH, TJ), axis=1).reshape(F, TJ)
    return jnp.concatenate([first, second], axis=1)


def body(features, inv_scales, inverse_tiles, tile_list, live_count):
    block = features[0, 0]
    live, places, inv = live_count.reshape(1), tile_list.reshape(2 * S), inv_scales.reshape(F, 1)
    cols = gather_row(block)
    near, far = gather_col(block)
    lhs, zi1 = prepare_pass(live, places, inv, near, far)
    swapped = swap_y(cols[:, F:])
    tiles = inverse_tiles[0, 0]
    carry, keep, send, held = tile_pass(False, live, places, inv, lhs, cols, near, far, tiles)
    got = swap_y(send)
    rpart, rpart2, cpart = tile_pass(True, live, places, inv, lhs, cols, zi1, swapped, carry, held)
    pair = (keep + got.astype(f32)).astype(bf16)
    cpart = lax.dynamic_update_slice(cpart, pair, (0, F, 0))
    total = scatter_row(cpart) + scatter_col(rpart, rpart2)
    return (jnp.square(inv_scales)[:, None] * total)[None, None]


def solution(mesh):
    return jax.shard_map(
        body,
        mesh=mesh,
        in_specs=(
            P("col", "row", None, None),
            P(),
            P("row", "col", None, None, None),
            P("row", "col", None, None),
            P("row", "col"),
        ),
        out_specs=P("col", "row", None, None),
        check_vma=False,
    )
```

```python
import jax
import jax.numpy as jnp
from jax import lax
from jax.experimental import pallas as pl
from jax.experimental.pallas import tpu as pltpu
from jax.sharding import PartitionSpec as P

F, TB, S, N = 32, 1024, 6, 16
HALF = N // 2
FH = F // 2
TJ = TB // 2
K = 48
SI, SUB, CJ = 512, 128, 256
NS = TB // SI
ROOT5 = 5.0**0.5
LOG2E = 1.4426950408889634
f32, bf16 = jnp.float32, jnp.bfloat16


def nn(a, b):
    return lax.dot_general(a, b, (((1,), (0,)), ((), ())), preferred_element_type=f32)


def nt(a, b):
    return lax.dot_general(a, b, (((1,), (1,)), ((), ())), preferred_element_type=f32)


def split3(q):
    a = q.astype(bf16)
    r = q - a.astype(f32)
    b = r.astype(bf16)
    c = (r - b.astype(f32)).astype(bf16)
    return jnp.concatenate([a, b, c], axis=0)


def scaled(iv, z):
    u = (iv * z.astype(f32)).astype(bf16)
    return u, split3(jnp.sum(jnp.square(u.astype(f32)), axis=0, keepdims=True))


def ones_row(width):
    return (lax.broadcasted_iota(jnp.int32, (K - F, width), 0) == 0).astype(bf16)


def row_place(list_ref, s):
    return col_slot(lax.shift_right_logical(list_ref[2 * s], 4) & 15, lax.axis_index("col"))


def prepare_rows(live_ref, list_ref, inv, near, far, lhs, zi1):
    iv = inv[...]

    @pl.loop(0, live_ref[0])
    def _(s):
        ib = row_place(list_ref, s)

        @pl.when(ib < HALF)
        def _():
            zi1[s, :F] = near[ib & 7]

        @pl.when(ib >= HALF)
        def _():
            zi1[s, :F] = far[ib & 7]

        zi1[s, F:] = ones_row(TB)
        u, q = scaled(iv, zi1[s, :F])
        pad = jnp.zeros((K - F - 6, TB), bf16)
        lhs[s] = jnp.concatenate([u, q, jnp.ones((3, TB), bf16), pad], axis=0).T


def tile_kernel(second, live_ref, list_ref, inv, lhs, cols, *refs):
    if second:
        zi1, swapped, carry, w, rout, rout2, cout, cacc, rhs, cb, racc = refs
    else:
        near, far, tiles, racc, keep, send, ahead, cacc, rhs, cb, w, sem = refs
    y = lax.axis_index("row") >> 3
    mine, other = pl.multiple_of(y * FH, FH), pl.multiple_of((1 - y) * FH, FH)
    live = live_ref[0]

    def fetch(s):
        return pltpu.make_async_copy(tiles.at[s, :, pl.ds(0, TJ)], w.at[s], sem.at[s])

    def fetch_ahead(s):
        return pltpu.make_async_copy(tiles.at[s, :, pl.ds(TJ, TJ)], ahead.at[s], sem.at[S + s])

    if not second:
        fetch(0).start()

        @pl.when(1 < live)
        def _():
            fetch(1).start()


    racc[...] = carry[...] if second else jnp.zeros(racc.shape, f32)
    cacc[...] = jnp.zeros(cacc.shape, f32)
    cb[NS - 1] = jnp.zeros((SI, TJ), bf16)
    iv = inv[...]

    def slot(s):
        big_i, big_j = list_ref[2 * s], list_ref[2 * s + 1]
        scale = jnp.where(big_i == big_j, 1.0, 2.0) * (-5.0 / 3.0 * ROOT5)
        return row_place(list_ref, s), big_j & 15, scale

    def z_of_i(s, ib, at):
        if second:
            return zi1[s, :F, at]
        return jnp.where(ib < HALF, near[ib & 7, :, at], far[ib & 7, :, at])

    def z_of_j(jb, js):
        if not second:
            return cols[jb, :F, js]
        a, b = cols[jb, F:, js], swapped[jb, :, js]
        return jnp.concatenate([jnp.where(y == 0, a, b), jnp.where(y == 0, b, a)], axis=0)

    def with_ones(z):
        return jnp.concatenate([z, ones_row(z.shape[1])], axis=0)

    def prepare(s, p):
        u, q = scaled(iv, z_of_j(list_ref[2 * s + 1] & 15, pl.ds(0, TJ)))
        pad = jnp.zeros((K - F - 6, TJ), bf16)
        rhs[p] = jnp.concatenate([u * bf16(-2.0), jnp.ones((3, TJ), bf16), q, pad], axis=0)

    def contract(n, jc, s, ib, jb, scale):
        js = pl.ds(jc * CJ, CJ)
        x, zj = cb[n, :, js], z_of_j(jb, js)
        ct = nn(with_ones(z_of_i(s, ib, pl.ds(n * SI, SI))), x)
        cacc[jb, :, js] += scale * (zj.astype(f32) * ct[F : F + 1] - ct[:F])
        return nt(with_ones(zj), x)

    def finish(n, s, ib, scale, rt):
        at = pl.ds(n * SI, SI)
        racc[ib, :, at] += scale * (z_of_i(s, ib, at).astype(f32) * rt[F : F + 1] - rt[:F])

    prepare(0, 0)

    @pl.loop(0, live)
    def _(s):
        p = s & 1
        prev = jnp.maximum(s - 1, 0)
        now, old = slot(s), slot(prev)
        if not second:
            fetch(s).wait()

            @pl.when(s + 2 < live)
            def _():
                fetch(s + 2).start()

            fetch_ahead(s).start()

        for n in range(NS):
            m, t, (ib, jb, scale) = (n - 1, s, now) if n else (NS - 1, prev, old)
            rt = None
            for jc in range(TJ // CJ):
                part = contract(m, jc, t, ib, jb, scale)
                rt = part if rt is None else rt + part
                js = pl.ds(jc * CJ, CJ)
                for h in range(SI // SUB):
                    at = pl.ds(n * SI + h * SUB, SUB)
                    sq = jnp.maximum(nn(lhs[s, at, :], rhs[p, :, js]), 1e-30)
                    d = sq * lax.rsqrt(sq)
                    e = jnp.exp2(d * (-ROOT5 * LOG2E))
                    g = ((d + 1.0 / ROOT5) * e).astype(bf16)
                    cb[n, h * SUB : (h + 1) * SUB, js] = g * w[s, at, js]
            finish(m, t, ib, scale, rt)
            if n == NS - 1:
                prepare(jnp.minimum(s + 1, live - 1), 1 - p)

    last = live - 1
    ib, jb, scale = slot(last)
    rt = None
    for jc in range(TJ // CJ):
        part = contract(NS - 1, jc, last, ib, jb, scale)
        rt = part if rt is None else rt + part
    finish(NS - 1, last, ib, scale, rt)
    if second:
        rout[...] = racc[:HALF].astype(bf16)
        rout2[...] = racc[HALF:].astype(bf16)
        cout[:, :F] = cacc[...].astype(bf16)
    else:
        keep[...] = cacc[:, pl.ds(mine, FH)]
        send[...] = cacc[:, pl.ds(other, FH)].astype(bf16)

        @pl.loop(0, live)
        def _(s):
            fetch_ahead(s).wait()


SMEM = pl.BlockSpec(memory_space=pltpu.SMEM)
VMEM = pl.BlockSpec(memory_space=pltpu.VMEM)


def prepare_pass(live, tile_list, inv, near, far):
    return pl.pallas_call(
        prepare_rows,
        out_shape=[jax.ShapeDtypeStruct((S, TB, K), bf16), jax.ShapeDtypeStruct((S, K, TB), bf16)],
        in_specs=[SMEM, SMEM] + [VMEM] * 3,
        out_specs=[VMEM] * 2,
        compiler_params=pltpu.CompilerParams(vmem_limit_bytes=16 * 1024 * 1024),
        cost_estimate=pl.CostEstimate(flops=2 * 10**9, bytes_accessed=10**6, transcendentals=0),
        name="prepare_rows",
    )(live, tile_list, inv, near, far)


def tile_pass(second, *args):
    total, tile = (N, F, TB), (S, TB, TJ)
    half = jax.ShapeDtypeStruct((HALF, F, TB), bf16)
    scratch = [
        pltpu.VMEM((N, F, TJ), f32),
        pltpu.VMEM((2, K, TJ), bf16),
        pltpu.VMEM((NS, SI, TJ), bf16),
    ]
    if second:
        outs = [half, half, jax.ShapeDtypeStruct((N, F + FH, TJ), bf16)]
        scratch.append(pltpu.VMEM(total, f32))
    else:
        scratch += [pltpu.VMEM(tile, bf16), pltpu.SemaphoreType.DMA((2 * S,))]
        outs = [(total, f32), ((N, FH, TJ), f32), ((N, FH, TJ), bf16), (tile, bf16)]
        outs = [jax.ShapeDtypeStruct(*out) for out in outs]

    def run(*refs):
        tile_kernel(second, *refs)

    return pl.pallas_call(
        run,
        out_shape=outs,
        in_specs=[SMEM] * 2 + [VMEM] * (len(args) - 3) + [VMEM if second else pl.BlockSpec(memory_space=pl.ANY)],
        out_specs=[VMEM] * len(outs),
        scratch_shapes=scratch,
        compiler_params=pltpu.CompilerParams(vmem_limit_bytes=40 * 1024 * 1024),
        cost_estimate=pl.CostEstimate(flops=10**10, bytes_accessed=10**7, transcendentals=0),
        name="second_half" if second else "first_half",
    )(*args)


def move(x, to):
    return lax.ppermute(x, "col", [(i, to(i)) for i in range(N)])


def along(k):
    return lambda i: (i + 4 * k) % N


def col_slot(owner, me):
    return ((owner ^ me) & 1) * HALF + (((me - owner + (owner & 3) - (me & 3)) & 12) >> 1) + (((owner ^ me) >> 1) & 1)


def gather_col(block):
    pair = jnp.stack([block, move(block, lambda i: i ^ 2)])
    mine = jnp.concatenate([pair] + [move(pair, along(k)) for k in (1, 2, 3)])
    return mine, move(mine, lambda i: i ^ 1)


def scatter_col(mine, other):
    chip = (mine.astype(f32) + move(other, lambda i: i ^ 1).astype(f32)).astype(bf16)
    pair = chip[:2].astype(f32)
    for k in (1, 2, 3):
        pair += move(chip[2 * k : 2 * k + 2], along(-k)).astype(f32)
    return pair[0] + move(pair[1].astype(bf16), lambda i: i ^ 2).astype(f32)


def swap_y(x):
    return lax.ppermute(x, "row", [(i, i ^ HALF) for i in range(N)])


def gather_row(block):
    whole = jnp.broadcast_to(block[None, :, :TJ], (N, F, TJ))
    part = jnp.broadcast_to(block[:, TJ:].reshape(2, 1, FH, TJ), (2, HALF, FH, TJ)).reshape(N, FH, TJ)
    return lax.all_to_all(jnp.concatenate([whole, part], axis=1), "row", 0, 0, tiled=True)


def scatter_row(parts):
    got = lax.all_to_all(parts, "row", 0, 0, tiled=True).astype(f32)
    second = jnp.sum(got[:, :F], axis=0)
    first = jnp.sum(got[:, F:].reshape(2, HALF, FH, TJ), axis=1).reshape(F, TJ)
    return jnp.concatenate([first, second], axis=1)


def body(features, inv_scales, inverse_tiles, tile_list, live_count):
    block = features[0, 0]
    live, places, inv = live_count.reshape(1), tile_list.reshape(2 * S), inv_scales.reshape(F, 1)
    cols = gather_row(block)
    near, far = gather_col(block)
    lhs, zi1 = prepare_pass(live, places, inv, near, far)
    swapped = swap_y(cols[:, F:])
    tiles = inverse_tiles[0, 0]
    carry, keep, send, ahead = tile_pass(False, live, places, inv, lhs, cols, near, far, tiles)
    got = swap_y(send)
    rpart, rpart2, cpart = tile_pass(True, live, places, inv, lhs, cols, zi1, swapped, carry, ahead)
    pair = (keep + got.astype(f32)).astype(bf16)
    cpart = lax.dynamic_update_slice(cpart, pair, (0, F, 0))
    total = scatter_row(cpart) + scatter_col(rpart, rpart2)
    return (jnp.square(inv_scales)[:, None] * total)[None, None]


def solution(mesh):
    return jax.shard_map(
        body,
        mesh=mesh,
        in_specs=(
            P("col", "row", None, None),
            P(),
            P("row", "col", None, None, None),
            P("row", "col", None, None),
            P("row", "col"),
        ),
        out_specs=P("col", "row", None, None),
        check_vma=False,
    )
```
